32 devices in a mesh: section: 4 (over y, x), shard: 8 (over z, core).
Axes of the slice: x: 2, y: 2, z: 4, core: 2. Of those that a mesh axis runs over, the one named last changes fastest.
Arguments:
- voltages: bfloat16 [4, 2, 1024, 32768], P('section', None, 'shard'), may hold values from -30 to 30, as said below
- feed_gains: bfloat16 [2, 1024, 1024], P(None, 'shard'), may hold values from -6 to 6
- grid_index: int32 [1024], replicated, may hold values from 0 to 1023, each once
- decay_rates: float32 [1024], P('shard'), may hold values from 0.3 to 0.95
- delays: int32 [1024, 512], replicated, may hold values from 0 to 4095
Outputs:
- dedispersed: bfloat16 [4, 7, 512, 2, 1024], P('section', None, None, None, 'shard')
The draws below stay inside these ranges and needn't reach their ends.
Inputs may be any that keep to these rules, and one draw needn't show every extreme that they name: Real sample voltages.
All inputs are finite; a program needn't handle non-finite values.
Results may differ from the reference program's by a relative error of at most 0.009.
Values may be sent and summed in bfloat16 or wider, within the bound.
No kernel may reach another device: no remote copies, remote signals or barrier semaphores. Data moves between devices by JAX's collectives and lax.ppermute only.
A program may use at most 192 MiB of HBM per device.

```python
import math
import jax
import jax.numpy as jnp
from jax import lax

POL = 2
GRID_X = 4
GRID_Y = 256
NSAMP = 2048
TDFT = 16
TRIALS = 512
FEEDS = 1024
CHANS = 1024
MODF = 7
BLOCKS = 4


def draw_voltages(key, part):
    key_noise = jax.random.fold_in(key, 11)
    key_level = jax.random.fold_in(key, 12)
    key_rise = jax.random.fold_in(key, 13)
    shape = (BLOCKS, POL, FEEDS, TDFT * NSAMP)
    jitter = jax.random.uniform(key_rise, (BLOCKS,), jnp.float32, 0.0, 1.0)
    block_rise = 3.0 ** ((jnp.arange(BLOCKS, dtype=jnp.float32) + jitter) / BLOCKS)
    block_rise = block_rise[:, None, None, None]
    feed_level = jnp.exp(jax.random.uniform(key_level, (1, POL, FEEDS, 1), jnp.float32, math.log(0.5), math.log(2.0)))
    fluctuation = jnp.clip(jax.random.normal(key_noise, shape, jnp.float32), -5.0, 5.0)
    return (fluctuation * block_rise * feed_level).astype(jnp.bfloat16)


def set_ends(entries, stream_key, least, largest):
    longest = entries.shape.index(max(entries.shape))
    spots = []
    for shift in (0, 1):
        where = [jax.random.randint(jax.random.fold_in(stream_key, axis), (), 0, length) for axis, length in enumerate(entries.shape)]
        where[longest] = (where[longest] + shift) % entries.shape[longest]
        spots.append(tuple(where))
    return entries.at[spots[0]].set(least).at[spots[1]].set(largest)


def block_levels(own_key, extent, pieces, low, top_value):
    def one(axis_at, parts):
        draws = jax.random.uniform(jax.random.fold_in(jax.random.fold_in(own_key, 6), axis_at), (parts,), jnp.float32, low / len(pieces), top_value / len(pieces))
        return jnp.repeat(jnp.exp(draws), extent[axis_at] // parts).reshape((-1,) + (1,) * (len(extent) - axis_at - 1))

    factor_of = one(*pieces[0])
    for cut in pieces[1:]:
        factor_of = factor_of * one(*cut)
    return factor_of


def centred(rng, extent, spread, limit, cuts=(), held_as=jnp.bfloat16):
    entries = jax.random.normal(rng, extent, jnp.float32) * spread
    if len(cuts) > 0:
        entries = block_levels(rng, extent, cuts, -0.22, 0.18) * entries
    return jnp.clip(entries, min=-limit, max=limit).astype(held_as)


def setup_inputs(seed: int = 0) -> dict:
    keys = jax.random.split(jax.random.key(seed), 6)
    voltages = draw_voltages(jax.random.fold_in(keys[5], 71), 0)
    feed_gains = centred(keys[1], (2, CHANS, FEEDS), 1.0, 6.0, ((1, 8),))
    grid_index = jax.random.permutation(keys[2], FEEDS).astype(jnp.int32)
    decay_rates = jnp.clip(0.3 + 0.65 * jax.random.uniform(keys[3], (CHANS,), jnp.float32) ** block_levels(keys[3], (CHANS,), ((0, 8),), -0.2, 0.2), 0.3, 0.95)
    delays = set_ends(jax.random.randint(keys[4], (CHANS, TRIALS), 0, 4096), jax.random.fold_in(keys[4], 1), 0, 4095).astype(jnp.int32)
    return {"voltages": voltages, "feed_gains": feed_gains, "grid_index": grid_index, "decay_rates": decay_rates, "delays": delays}


def spectral_table():
    row_index = jnp.arange(CHANS, dtype=jnp.int32)[:, None]
    col_index = jnp.arange(NSAMP, dtype=jnp.int32)[None, :]
    angles = 2.0 * math.pi / NSAMP * (row_index * col_index % NSAMP).astype(jnp.float32)
    return jnp.concatenate([jnp.cos(angles), -jnp.sin(angles)], 0).astype(jnp.bfloat16)

def twiddle_table(length):
    row_index = jnp.arange(length, dtype=jnp.int32)[:, None]
    col_index = jnp.arange(length, dtype=jnp.int32)[None, :]
    angles = 2.0 * math.pi / length * (row_index * col_index % length).astype(jnp.float32)
    cosine = jnp.cos(angles)
    sine = jnp.sin(angles)
    return jnp.stack([jnp.stack([cosine, -sine], 1), jnp.stack([sine, cosine], 1)], 0)

def frame_table():
    frames = jnp.arange(TDFT, dtype=jnp.int32)[:, None]
    freqs = jnp.arange(1, MODF + 1, dtype=jnp.int32)[None, :]
    angles = 2.0 * math.pi / TDFT * (frames * freqs % TDFT).astype(jnp.float32)
    return jnp.concatenate([jnp.cos(angles), -jnp.sin(angles)], 1) / math.sqrt(TDFT)

def form_beams(transposed_block, feed_gains, cell_feed):
    chan_count = transposed_block.shape[1]
    pol_count = transposed_block.shape[2]
    values = transposed_block.reshape(2, chan_count, pol_count, FEEDS, TDFT).astype(jnp.float32)
    gain_values = feed_gains.astype(jnp.float32)[:, :, None, :, None]
    real_part = gain_values[0] * values[0] - gain_values[1] * values[1]
    imag_part = gain_values[0] * values[1] + gain_values[1] * values[0]
    calibrated = jnp.stack([real_part, imag_part]).astype(jnp.bfloat16)
    gridded = jnp.take(calibrated, cell_feed, axis=3).reshape(2, chan_count, pol_count, GRID_X, GRID_Y, TDFT)
    rows = twiddle_table(GRID_Y).astype(jnp.bfloat16)
    row_beams = jnp.einsum('acpxyn,aybw->bcpxwn', gridded.astype(jnp.float32), rows.astype(jnp.float32))
    beam_voltage = jnp.einsum('bcpxwn,bxeu->ecpnuw', row_beams, twiddle_table(GRID_X), precision=lax.Precision.HIGHEST)
    powers = lax.optimization_barrier(jnp.sum(beam_voltage * beam_voltage, axis=0))
    return jnp.moveaxis(powers, 1, 0).reshape(pol_count, chan_count, TDFT, FEEDS)

def dedisperse(modulated, delays):

    def per_frequency(position_index):
        frequency = position_index + 1
        angles = 2.0 * math.pi / TDFT * (frequency * delays % TDFT).astype(jnp.float32)
        phases = jnp.concatenate([jnp.cos(angles), jnp.sin(angles)], 0).astype(jnp.bfloat16)
        mod_real = modulated[:, :, position_index]
        modulated_imaginary = modulated[:, :, MODF + position_index]
        stacked = jnp.concatenate([jnp.concatenate([mod_real, modulated_imaginary], 1), jnp.concatenate([modulated_imaginary, -mod_real], 1)], 0)
        result = lax.dot_general(phases, stacked, (((0,), (0,)), ((), ())), preferred_element_type=jnp.float32) / math.sqrt(CHANS)
        return result.reshape(TRIALS, 2, modulated.shape[1]).astype(jnp.bfloat16)
    return lax.map(per_frequency, jnp.arange(MODF, dtype=jnp.int32))

def reference(voltages, feed_gains, grid_index, decay_rates, delays):
    cell_feed = jnp.zeros((FEEDS,), jnp.int32).at[grid_index].set(jnp.arange(FEEDS, dtype=jnp.int32))
    spectral_rows = spectral_table()

    def block_energy(block_volts):
        samples = block_volts.reshape(POL * FEEDS * TDFT, NSAMP)
        spectra = lax.dot_general(spectral_rows, samples, (((1,), (1,)), ((), ())), preferred_element_type=jnp.float32)
        spectra = (spectra * (1.0 / math.sqrt(NSAMP))).astype(jnp.bfloat16).reshape(2, CHANS, POL, FEEDS * TDFT)
        return lax.optimization_barrier(jnp.sum(form_beams(spectra, feed_gains, cell_feed), axis=0))
    beam_power = lax.map(block_energy, voltages)
    levels = lax.optimization_barrier(jnp.mean(beam_power, axis=(2, 3))) + 1e-06
    ratio_dividend = jnp.zeros((CHANS,), jnp.float32)
    ratio_divisor = jnp.zeros((CHANS,), jnp.float32)
    baseline_levels = []
    for block in range(BLOCKS):
        ratio_dividend = decay_rates * ratio_dividend + levels[block]
        ratio_divisor = decay_rates * ratio_divisor + 1.0
        baseline_levels.append(ratio_dividend / ratio_divisor)
    baseline_level = jnp.stack(baseline_levels)

    def finish(inputs):
        block_power_values, block_base = inputs
        normalized = block_power_values / block_base[:, None, None] - 1.0
        modulated = jnp.einsum('cnb,nq->cbq', normalized, frame_table(), precision=lax.Precision.HIGHEST).astype(jnp.bfloat16)
        return dedisperse(modulated, delays)
    return lax.map(finish, (beam_power, baseline_level))
```

```python
import functools
import math

import jax
import jax.numpy as jnp
import numpy as np
from jax import lax
from jax.experimental import pallas as pl
from jax.experimental.pallas import tpu as pltpu
from jax.sharding import PartitionSpec as P

POL = 2
GRID_X = 4
GRID_Y = 256
NSAMP = 2048
MODF = 7
LANES = 128
ROWS = 16


def spectral_constant(chans):
    row_index = np.arange(chans, dtype=np.int64)[:, None]
    col_index = np.arange(NSAMP, dtype=np.int64)[None, :]
    angles = np.float32(2.0 * math.pi / NSAMP) * (row_index * col_index % NSAMP).astype(np.float32)
    return np.stack([np.cos(angles), -np.sin(angles)], 0).astype(np.float32).astype(jnp.bfloat16)


def cosine_of(index, period):
    half, quarter = period // 2, period // 4
    folded = jnp.abs(((index + half) & (period - 1)) - half) - quarter
    x = folded.astype(jnp.float32) * np.float32(2.0 * math.pi / period)
    x2 = x * x
    series = np.float32(-1.0 / math.factorial(11))
    for order in (9, 7, 5, 3, 1):
        sign = 1.0 if order % 4 == 1 else -1.0
        series = series * x2 + np.float32(sign / math.factorial(order))
    return -x * series


def beam_table(grid_index):
    feeds = grid_index.shape[0]
    cell = jnp.concatenate([grid_index, grid_index])[:, None]
    part = lax.broadcasted_iota(jnp.int32, (2 * feeds, 1), 0) // feeds
    column = lax.broadcasted_iota(jnp.int32, (1, 2 * feeds), 1)
    end = (column // LANES) % 2
    beam = column // (2 * LANES) * LANES + column % LANES
    x, y = cell // GRID_Y, cell % GRID_Y
    u, w = beam // GRID_Y, beam % GRID_Y
    turn = y * w + (GRID_Y // GRID_X) * (x * u) + (GRID_Y // 4) * (end - part)
    return cosine_of(turn, GRID_Y).astype(jnp.bfloat16)


def frame_sums(frames):
    even = [frames[n] + frames[n + 8] for n in range(8)]
    odd = [frames[n] - frames[n + 8] for n in range(8)]
    ee = [even[n] + even[n + 4] for n in range(4)]
    ed = [even[n] - even[n + 4] for n in range(4)]
    real, imag = [None] * 8, [None] * 8
    real[4] = ee[0] - ee[2]
    imag[4] = ee[3] - ee[1]
    root = np.float32(math.sqrt(0.5))
    diff, total = root * (ed[1] - ed[3]), root * (ed[1] + ed[3])
    real[2], imag[2] = ed[0] + diff, -ed[2] - total
    real[6], imag[6] = ed[0] - diff, ed[2] - total
    minus = [None] + [odd[n] - odd[8 - n] for n in (1, 2, 3)]
    plus = [None] + [odd[n] + odd[8 - n] for n in (1, 2, 3)]
    for f in (1, 3, 5, 7):
        c = [np.float32(math.cos(math.pi * f * n / 8)) for n in range(4)]
        s = [np.float32(math.sin(math.pi * f * n / 8)) for n in range(5)]
        real[f] = odd[0] + (c[1] * minus[1] + c[2] * minus[2] + c[3] * minus[3])
        last = odd[4] if s[4] > 0 else -odd[4]
        imag[f] = -(last + (s[1] * plus[1] + s[2] * plus[2] + s[3] * plus[3]))
    return [np.float32(0.25) * v for v in real[1:] + imag[1:]]


def channelize_kernel(shards, size, frames, n_after, place, table, volts, *rest):
    outs, (held,) = rest[n_after : n_after + shards], rest[n_after + shards + 1 :]
    rest[n_after + shards][...] = jnp.zeros((8, LANES), jnp.int32)
    for n in range(frames):
        samples = volts[0, :, :, n * NSAMP : (n + 1) * NSAMP].reshape(-1, NSAMP)
        product = lax.dot_general(
            table[...], samples, (((1,), (1,)), ((), ())), preferred_element_type=jnp.float32
        )
        held[...] = (product * np.float32(1.0 / math.sqrt(NSAMP))).reshape(held.shape)
        for m in range(shards):
            mine = held[place[0] ^ m].astype(jnp.bfloat16)
            for a in range(2):
                for p in range(POL):
                    outs[m][a, p, n] = mine[a * size : (a + 1) * size, p * LANES : (p + 1) * LANES]


def channelize(place, table, voltages, size, shards, after):
    total = voltages.shape[3] // NSAMP
    frames = 2 if size < 32 else 4
    shape = (2, POL, total, size, LANES)
    block = (2, POL, frames, size, LANES)
    outs = pl.pallas_call(
        functools.partial(channelize_kernel, shards, size, frames, len(after)),
        grid_spec=pltpu.PrefetchScalarGridSpec(
            num_scalar_prefetch=1,
            grid=(total // frames,),
            in_specs=[
                pl.BlockSpec(table.shape, lambda n, _: (0, 0)),
                pl.BlockSpec((1, POL, LANES, frames * NSAMP), lambda n, _: (0, 0, 0, n)),
            ]
            + [pl.BlockSpec(memory_space=pl.ANY)] * len(after),
            out_specs=[pl.BlockSpec(block, lambda n, _: (0, 0, n, 0, 0))] * shards
            + [pl.BlockSpec((8, LANES), lambda n, _: (0, 0))],
            scratch_shapes=[pltpu.VMEM((shards, 2 * size, POL * LANES), jnp.float32)],
        ),
        out_shape=[jax.ShapeDtypeStruct(shape, jnp.bfloat16)] * shards
        + [jax.ShapeDtypeStruct((8, LANES), jnp.int32)],
        compiler_params=pltpu.CompilerParams(vmem_limit_bytes=40 << 20),
        cost_estimate=pl.CostEstimate(
            flops=2 * table.shape[0] * NSAMP * POL * LANES * total,
            bytes_accessed=voltages.size * 2 + table.size * 4,
            transcendentals=0,
        ),
        name="channelize",
    )(place, table, voltages, *after)
    return outs[:shards], outs[shards]


def beam_kernel(shards, frames, place, gains, table, *rest):
    spectra, outs, level, held = rest[:shards], rest[shards : 2 * shards], rest[-2], rest[-1]
    feeds = shards * LANES
    rows = POL * frames * ROWS
    for m in range(shards):
        at = pl.multiple_of((place[0] ^ m) * LANES, LANES)
        gain_real = gains[0, :, pl.ds(at, LANES)].astype(jnp.float32)
        gain_imag = gains[1, :, pl.ds(at, LANES)].astype(jnp.float32)
        real = spectra[m][0].astype(jnp.float32)
        imag = spectra[m][1].astype(jnp.float32)
        cal_real = (gain_real * real - gain_imag * imag).astype(jnp.bfloat16)
        cal_imag = (gain_real * imag + gain_imag * real).astype(jnp.bfloat16)
        held[:, pl.ds(at, LANES)] = cal_real.reshape(rows, LANES)
        held[:, pl.ds(pl.multiple_of(at + feeds, LANES), LANES)] = cal_imag.reshape(rows, LANES)
    sums = jnp.zeros((ROWS, LANES), jnp.float32)
    for m in range(shards):
        at = pl.multiple_of((place[0] ^ m) * (2 * LANES), 2 * LANES)
        beams = jnp.dot(held[...], table[:, pl.ds(at, 2 * LANES)], preferred_element_type=jnp.float32)
        squares = beams * beams
        power = squares[:, :LANES] + squares[:, LANES:]
        power = (power[: rows // 2] + power[rows // 2 :]).reshape(frames, ROWS, LANES)
        sums = sums + jnp.sum(power, axis=0)
        for q, value in enumerate(frame_sums(power)):
            outs[m][q] = value
    level[...] = sums


def form_beams(place, gains, table, spectra, start, size, frames):
    shards = len(spectra)
    outs = pl.pallas_call(
        functools.partial(beam_kernel, shards, frames),
        grid_spec=pltpu.PrefetchScalarGridSpec(
            num_scalar_prefetch=1,
            grid=(size // ROWS,),
            in_specs=[
                pl.BlockSpec((2, ROWS, gains.shape[2]), lambda g, _: (0, start // ROWS + g, 0)),
                pl.BlockSpec(table.shape, lambda g, _: (0, 0), pipeline_mode=pl.Buffered(1)),
            ]
            + [pl.BlockSpec((2, POL, frames, ROWS, LANES), lambda g, _: (0, 0, 0, g, 0))] * shards,
            out_specs=[pl.BlockSpec((2 * MODF, ROWS, LANES), lambda g, _: (0, g, 0))] * shards
            + [pl.BlockSpec((ROWS, LANES), lambda g, _: (g, 0))],
            scratch_shapes=[pltpu.VMEM((POL * frames * ROWS, table.shape[0]), jnp.bfloat16)],
        ),
        out_shape=[jax.ShapeDtypeStruct((2 * MODF, size, LANES), jnp.float32)] * shards
        + [jax.ShapeDtypeStruct((size, LANES), jnp.float32)],
        compiler_params=pltpu.CompilerParams(vmem_limit_bytes=46 << 20),
        cost_estimate=pl.CostEstimate(
            flops=2 * POL * frames * size * table.size,
            bytes_accessed=table.size * 2 + 8 * size * frames * gains.shape[2],
            transcendentals=0,
        ),
        name="form_beams",
    )(place, gains, table, *spectra)
    return outs[:shards], outs[shards]


def normalise_kernel(count, scale, section, levels, decay, *rest):
    shards = (len(rest)) // 2
    rate = decay[...]
    dividend, divisor = jnp.zeros_like(rate), jnp.zeros_like(rate)
    for block in range(count):
        mean = jnp.sum(levels[block], axis=1, keepdims=True) * scale + np.float32(1e-6)
        later = block <= section[0]
        dividend = jnp.where(later, rate * dividend + mean, dividend)
        divisor = jnp.where(later, rate * divisor + 1.0, divisor)
    inverse = divisor / dividend
    for m in range(shards):
        rest[shards + m][...] = (rest[m][...] * inverse).astype(jnp.bfloat16)


def normalise(section, levels, decay, sums, scale):
    spec = pl.BlockSpec(memory_space=pltpu.VMEM)
    return pl.pallas_call(
        functools.partial(normalise_kernel, levels.shape[0], scale),
        in_specs=[pl.BlockSpec(memory_space=pltpu.SMEM)] + [spec] * (2 + len(sums)),
        out_specs=[spec] * len(sums),
        out_shape=[jax.ShapeDtypeStruct(s.shape, jnp.bfloat16) for s in sums],
        compiler_params=pltpu.CompilerParams(vmem_limit_bytes=24 << 20),
        name="normalise",
    )(section, levels, decay, *sums)


def dedisperse_kernel(shards, size, last, first, scale, place, cosine, sine, *rest):
    parts = rest[:shards]
    total = None if first else rest[shards]
    out, real, imag = rest[-3:]
    f = pl.program_id(0)
    for m in range(shards):
        at = pl.multiple_of((place[0] ^ m) * size, size)
        real[pl.ds(at, size), :] = parts[m][f]
        imag[pl.ds(at, size), :] = parts[m][f + MODF]
    value = jnp.dot(cosine[0], real[...], preferred_element_type=jnp.float32) + jnp.dot(
        sine[0], imag[...], preferred_element_type=jnp.float32
    )
    if total is not None:
        value = value + total[0]
    out[0] = (value * scale).astype(out.dtype) if last else value


def dedisperse(place, cosine, sine, parts, total, last, scale):
    shards, (_, size, _) = len(parts), parts[0].shape
    rows, depth = cosine.shape[1:]
    each = lambda f, _: (f, 0, 0)
    whole = pl.BlockSpec(parts[0].shape, lambda f, _: (0, 0, 0))
    sums = [] if total is None else [total]
    return pl.pallas_call(
        functools.partial(dedisperse_kernel, shards, size, last, total is None, scale),
        grid_spec=pltpu.PrefetchScalarGridSpec(
            num_scalar_prefetch=1,
            grid=(MODF,),
            in_specs=[pl.BlockSpec((1, rows, depth), each)] * 2
            + [whole] * shards
            + [pl.BlockSpec((1, rows, LANES), each)] * len(sums),
            out_specs=pl.BlockSpec((1, rows, LANES), each),
            scratch_shapes=[pltpu.VMEM((depth, LANES), jnp.bfloat16)] * 2,
        ),
        out_shape=jax.ShapeDtypeStruct((MODF, rows, LANES), jnp.bfloat16 if last else jnp.float32),
        compiler_params=pltpu.CompilerParams(vmem_limit_bytes=32 << 20),
        cost_estimate=pl.CostEstimate(
            flops=4 * MODF * rows * depth * LANES,
            bytes_accessed=4 * MODF * rows * (depth + LANES),
            transcendentals=0,
        ),
        name="dedisperse",
    )(place, cosine, sine, *parts, *sums)


def phase_tables(turns, frames):
    delay, quarter = turns
    f = jnp.arange(1, MODF + 1, dtype=jnp.int32)[:, None, None]
    turn = f * delay[None] + quarter[None]
    cosine = cosine_of(turn, frames).astype(jnp.bfloat16)
    sine = cosine_of(turn - frames // 4, frames).astype(jnp.bfloat16)
    return cosine, sine


def chunk_sizes(channels):
    edge, inner = ROWS, 2 * ROWS
    if channels < 2 * edge + inner:
        return [ROWS] * (channels // ROWS)
    left = channels - 2 * edge
    sizes = [edge] + [inner] * (left // inner) + ([left % inner] if left % inner else []) + [edge]
    return sizes


def pipelined(voltages, feed_gains, grid_index, decay_rates, delays):
    shards, blocks = lax.axis_size("shard"), lax.axis_size("section")
    frames = voltages.shape[3] // NSAMP
    chans, trials = delays.shape
    feeds = grid_index.shape[0]
    local = chans // shards
    place = lax.axis_index("shard").reshape(1)
    section = lax.axis_index("section").reshape(1)
    sizes = chunk_sizes(local)
    starts = [sum(sizes[:c]) for c in range(len(sizes))]
    rows = spectral_constant(chans).reshape(2, shards, local, NSAMP)
    scale = np.float32(1.0 / (frames * feeds))

    def exchange(parts):
        got = [parts[0]] + [None] * (shards - 1)
        order = [m for m in range(shards - 1, 0, -1)]
        for m in order:
            got[m] = lax.ppermute(parts[m], "shard", [(j, j ^ m) for j in range(shards)])
        return got

    def send_spectra(c, after):
        table = np.ascontiguousarray(rows[:, :, starts[c] : starts[c] + sizes[c]].transpose(1, 0, 2, 3))
        table = jnp.asarray(table.reshape(-1, NSAMP))
        parts, zero = channelize(place, table, voltages, sizes[c], shards, after)
        return exchange(parts), zero

    received, zero = {}, None
    received[0], zero = send_spectra(0, [])
    received[1], _ = send_spectra(1, [])

    zero = zero[0, 0]
    table = beam_table(grid_index + zero)
    by_trial = jnp.transpose((delays + zero) & (frames - 1)).reshape(trials, shards, local)
    by_trial = jnp.repeat(by_trial, 2, axis=0)
    quarter = (lax.broadcasted_iota(jnp.int32, (2 * trials, 1), 0) % 2) * (frames // 4)

    total = None
    pending = None
    for c in range(len(sizes)):
        start, size = starts[c], sizes[c]
        if c + 2 < len(sizes):
            received[c + 2], _ = send_spectra(c + 2, received[c][1:])
        sums, level = form_beams(place, feed_gains, table, received[c], start, size, frames)
        levels = lax.all_gather(level, "section")
        decay = decay_rates[start : start + size].reshape(size, 1)
        modulated = exchange(normalise(section, levels, decay, sums, scale))
        chosen = by_trial[:, :, start : start + size].reshape(2 * trials, shards * size)
        cosine, sine = phase_tables((chosen, quarter), frames)
        total = dedisperse(
            place, cosine, sine, modulated, total, c + 1 == len(sizes), np.float32(1.0 / math.sqrt(chans))
        )
    return total.reshape(1, MODF, trials, 2, feeds // shards)


def plain(voltages, feed_gains, grid_index, decay_rates, delays):
    shards = lax.axis_size("shard")
    chans, trials = delays.shape
    feeds, local_feeds = grid_index.shape[0], voltages.shape[2]
    frames = voltages.shape[3] // NSAMP
    samples = voltages[0].reshape(POL * local_feeds * frames, NSAMP)
    rows = jnp.asarray(spectral_constant(chans).reshape(2 * chans, NSAMP))
    spectra = lax.dot_general(rows, samples, (((1,), (1,)), ((), ())), preferred_element_type=jnp.float32)
    spectra = (spectra * (1.0 / math.sqrt(NSAMP))).astype(jnp.bfloat16)
    spectra = spectra.reshape(2, chans, POL, local_feeds, frames)
    turned = lax.all_to_all(spectra, "shard", split_axis=1, concat_axis=3, tiled=True)
    values = turned.astype(jnp.float32)
    gain = feed_gains.astype(jnp.float32)[:, :, None, :, None]
    calibrated = jnp.stack(
        [gain[0] * values[0] - gain[1] * values[1], gain[0] * values[1] + gain[1] * values[0]]
    ).astype(jnp.bfloat16)
    table = beam_table(grid_index).reshape(2, feeds, feeds // LANES, 2, LANES)
    beams = jnp.einsum("akpfn,afdel->eknpdl", calibrated, table, preferred_element_type=jnp.float32)
    power = jnp.sum(beams * beams, axis=(0, 3)).reshape(-1, frames, feeds)
    levels = jnp.mean(power, axis=(1, 2)) + 1e-06
    gathered = lax.all_gather(levels, "section")
    dividend, divisor = jnp.zeros_like(levels), jnp.zeros_like(levels)
    for block in range(gathered.shape[0]):
        later = block <= lax.axis_index("section")
        dividend = jnp.where(later, decay_rates * dividend + gathered[block], dividend)
        divisor = jnp.where(later, decay_rates * divisor + 1.0, divisor)
    power = power * (divisor / dividend)[:, None, None]
    sums = jnp.stack(frame_sums([power[:, n] for n in range(frames)])).astype(jnp.bfloat16)
    moved = lax.all_to_all(sums, "shard", split_axis=2, concat_axis=1, tiled=True)
    turn = jnp.arange(1, MODF + 1, dtype=jnp.int32)[:, None, None] * (delays & (frames - 1))[None]
    cosine = cosine_of(turn, frames).astype(jnp.bfloat16)
    sine = cosine_of(turn - frames // 4, frames).astype(jnp.bfloat16)
    dot = functools.partial(jnp.einsum, "fkt,fkb->ftb", preferred_element_type=jnp.float32)
    real, imag = moved[:MODF], moved[MODF:]
    result = jnp.stack(
        [dot(cosine, real) + dot(sine, imag), dot(cosine, imag) - dot(sine, real)], 2
    ) * (1.0 / math.sqrt(chans))
    return result.astype(jnp.bfloat16)[None]


def solution(mesh):
    def shards(voltages, feed_gains, grid_index, decay_rates, delays):
        count = lax.axis_size("shard")
        fits = (
            voltages.shape[2] == LANES
            and grid_index.shape[0] == count * LANES
            and delays.shape[0] % (count * ROWS) == 0
            and voltages.shape[3] == ROWS * NSAMP
            and count & (count - 1) == 0
            and delays.shape[0] // count >= 2 * ROWS
        )
        form = pipelined if fits else plain
        return form(voltages, feed_gains, grid_index, decay_rates, delays)

    in_specs = (P("section", None, "shard", None), P(None, "shard", None), P(), P("shard"), P())
    out_specs = P("section", None, None, None, "shard")
    return jax.shard_map(shards, mesh=mesh, in_specs=in_specs, out_specs=out_specs, check_vma=False)
```

```python
import functools
import math

import jax
import jax.numpy as jnp
import numpy as np
from jax import lax
from jax.experimental import pallas as pl
from jax.experimental.pallas import tpu as pltpu
from jax.sharding import PartitionSpec as P

POL = 2
GRID_X = 4
GRID_Y = 256
NSAMP = 2048
MODF = 7
LANES = 128
ROWS = 16
COST = pl.CostEstimate(flops=1000, bytes_accessed=1000, transcendentals=0)
TOKEN = jax.ShapeDtypeStruct((8, LANES), jnp.int32)
VMEM = 60 << 20


def spectral_constant(chans):
    row_index = np.arange(chans, dtype=np.int64)[:, None]
    col_index = np.arange(NSAMP, dtype=np.int64)[None, :]
    angles = np.float32(2.0 * math.pi / NSAMP) * (row_index * col_index % NSAMP).astype(np.float32)
    return np.stack([np.cos(angles), -np.sin(angles)], 0).astype(np.float32).astype(jnp.bfloat16)


def cosine_of(index, period):
    half, quarter = period // 2, period // 4
    folded = jnp.abs(((index + half) & (period - 1)) - half) - quarter
    x = folded.astype(jnp.float32) * np.float32(2.0 * math.pi / period)
    x2 = x * x
    series = np.float32(-1.0 / math.factorial(11))
    for order in (9, 7, 5, 3, 1):
        sign = 1.0 if order % 4 == 1 else -1.0
        series = series * x2 + np.float32(sign / math.factorial(order))
    return -x * series


def beam_table(grid_index):
    feeds = grid_index.shape[0]
    cell = jnp.concatenate([grid_index, grid_index])[:, None]
    part = lax.broadcasted_iota(jnp.int32, (2 * feeds, 1), 0) // feeds
    column = lax.broadcasted_iota(jnp.int32, (1, 2 * feeds), 1)
    end = (column // LANES) % 2
    beam = column // (2 * LANES) * LANES + column % LANES
    x, y = cell // GRID_Y, cell % GRID_Y
    u, w = beam // GRID_Y, beam % GRID_Y
    turn = y * w + (GRID_Y // GRID_X) * (x * u) + (GRID_Y // 4) * (end - part)
    return cosine_of(turn, GRID_Y).astype(jnp.bfloat16)


def frame_sums(frames):
    even = [frames[n] + frames[n + 8] for n in range(8)]
    odd = [frames[n] - frames[n + 8] for n in range(8)]
    ee = [even[n] + even[n + 4] for n in range(4)]
    ed = [even[n] - even[n + 4] for n in range(4)]
    real, imag = [None] * 8, [None] * 8
    real[4] = ee[0] - ee[2]
    imag[4] = ee[3] - ee[1]
    root = np.float32(math.sqrt(0.5))
    diff, total = root * (ed[1] - ed[3]), root * (ed[1] + ed[3])
    real[2], imag[2] = ed[0] + diff, -ed[2] - total
    real[6], imag[6] = ed[0] - diff, ed[2] - total
    minus = [None] + [odd[n] - odd[8 - n] for n in (1, 2, 3)]
    plus = [None] + [odd[n] + odd[8 - n] for n in (1, 2, 3)]
    for f in (1, 3, 5, 7):
        c = [np.float32(math.cos(math.pi * f * n / 8)) for n in range(4)]
        s = [np.float32(math.sin(math.pi * f * n / 8)) for n in range(5)]
        real[f] = odd[0] + (c[1] * minus[1] + c[2] * minus[2] + c[3] * minus[3])
        last = odd[4] if s[4] > 0 else -odd[4]
        imag[f] = -(last + (s[1] * plus[1] + s[2] * plus[2] + s[3] * plus[3]))
    return [np.float32(0.25) * v for v in real[1:] + imag[1:]]


def slots(shards):
    return [m for m in range(shards // 2, shards)] + [m for m in range(shards // 2 - 1, -1, -1)]


def channelize_kernel(shards, size, frames, n_after, place, table, volts, *rest):
    outs, zero, held = rest[n_after : n_after + shards], rest[-2], rest[-1]
    zero[...] = jnp.zeros((8, LANES), jnp.int32)
    for n in range(frames):
        samples = volts[0, :, :, n * NSAMP : (n + 1) * NSAMP].reshape(-1, NSAMP)
        product = lax.dot_general(
            table[...], samples, (((1,), (1,)), ((), ())), preferred_element_type=jnp.float32
        )
        held[...] = (product * np.float32(1.0 / math.sqrt(NSAMP))).reshape(held.shape)
        for out, m in zip(outs, slots(shards)):
            mine = held[place[0] ^ m].astype(jnp.bfloat16)
            for a in range(2):
                for p in range(POL):
                    out[a, p, n] = mine[a * size : (a + 1) * size, p * LANES : (p + 1) * LANES]


def channelize(place, table, voltages, size, shards, after):
    total = voltages.shape[3] // NSAMP
    frames = 2 if size < 32 else 4
    shape = (2, POL, total, size, LANES)
    block = (2, POL, frames, size, LANES)
    outs = pl.pallas_call(
        functools.partial(channelize_kernel, shards, size, frames, len(after)),
        grid_spec=pltpu.PrefetchScalarGridSpec(
            num_scalar_prefetch=1,
            grid=(total // frames,),
            in_specs=[
                pl.BlockSpec(table.shape, lambda n, _: (0, 0)),
                pl.BlockSpec((1, POL, LANES, frames * NSAMP), lambda n, _: (0, 0, 0, n)),
            ]
            + [pl.BlockSpec(memory_space=pl.ANY)] * len(after),
            out_specs=[pl.BlockSpec(block, lambda n, _: (0, 0, n, 0, 0))] * shards
            + [pl.BlockSpec((8, LANES), lambda n, _: (0, 0))],
            scratch_shapes=[pltpu.VMEM((shards, 2 * size, POL * LANES), jnp.float32)],
        ),
        out_shape=[jax.ShapeDtypeStruct(shape, jnp.bfloat16)] * shards
        + [jax.ShapeDtypeStruct((8, LANES), jnp.int32)],
        compiler_params=pltpu.CompilerParams(vmem_limit_bytes=VMEM),
        cost_estimate=COST,
        name="channelize",
    )(place, table, voltages, *after)
    return outs[:-1], outs[-1]


def beam_kernel(shards, frames, place, gains, table, *rest):
    outs, level, held = rest[-2 - shards : -2], rest[-2], rest[-1]
    feeds = shards * LANES
    rows = POL * frames * ROWS
    for spectra, m in zip(rest, slots(shards)):
        at = pl.multiple_of((place[0] ^ m) * LANES, LANES)
        gain_real = gains[0, :, pl.ds(at, LANES)].astype(jnp.float32)
        gain_imag = gains[1, :, pl.ds(at, LANES)].astype(jnp.float32)
        real = spectra[0].astype(jnp.float32)
        imag = spectra[1].astype(jnp.float32)
        cal_real = (gain_real * real - gain_imag * imag).astype(jnp.bfloat16)
        cal_imag = (gain_real * imag + gain_imag * real).astype(jnp.bfloat16)
        held[:, pl.ds(at, LANES)] = cal_real.reshape(rows, LANES)
        held[:, pl.ds(pl.multiple_of(at + feeds, LANES), LANES)] = cal_imag.reshape(rows, LANES)
    sums = jnp.zeros((ROWS, LANES), jnp.float32)
    for out, m in zip(outs, slots(shards)):
        at = pl.multiple_of((place[0] ^ m) * (2 * LANES), 2 * LANES)
        beams = jnp.dot(held[...], table[:, pl.ds(at, 2 * LANES)], preferred_element_type=jnp.float32)
        squares = beams * beams
        power = squares[:, :LANES] + squares[:, LANES:]
        power = (power[: rows // 2] + power[rows // 2 :]).reshape(frames, ROWS, LANES)
        sums = sums + jnp.sum(power, axis=0)
        for q, value in enumerate(frame_sums(power)):
            out[q] = value
    level[...] = sums


def form_beams(place, gains, table, spectra, start, size, frames, after):
    shards = len(spectra)
    block = (2, POL, frames, ROWS, LANES)
    outs = pl.pallas_call(
        functools.partial(beam_kernel, shards, frames),
        grid_spec=pltpu.PrefetchScalarGridSpec(
            num_scalar_prefetch=1,
            grid=(size // ROWS,),
            in_specs=[
                pl.BlockSpec((2, ROWS, gains.shape[2]), lambda g, _: (0, start // ROWS + g, 0)),
                pl.BlockSpec(table.shape, lambda g, _: (0, 0), pipeline_mode=pl.Buffered(1)),
            ]
            + [pl.BlockSpec(block, lambda g, _: (0, 0, 0, g, 0))] * shards
            + [pl.BlockSpec(memory_space=pl.ANY)] * len(after),
            out_specs=[pl.BlockSpec((2 * MODF, ROWS, LANES), lambda g, _: (0, g, 0))] * shards
            + [pl.BlockSpec((ROWS, LANES), lambda g, _: (g, 0))],
            scratch_shapes=[pltpu.VMEM((POL * frames * ROWS, table.shape[0]), jnp.bfloat16)],
        ),
        out_shape=[jax.ShapeDtypeStruct((2 * MODF, size, LANES), jnp.float32)] * shards
        + [jax.ShapeDtypeStruct((size, LANES), jnp.float32)],
        compiler_params=pltpu.CompilerParams(vmem_limit_bytes=VMEM),
        cost_estimate=COST,
        name="form_beams",
    )(place, gains, table, *spectra, *after)
    return outs[:-1], outs[-1]


def normalise_kernel(count, chips, scale, section, levels, decay, *rest):
    rate = decay[...]
    dividend, divisor = jnp.zeros_like(rate), jnp.zeros_like(rate)
    for block in range(count):
        mean = jnp.sum(levels[block], axis=1, keepdims=True) * scale + np.float32(1e-6)
        later = block <= section[0]
        dividend = jnp.where(later, rate * dividend + mean, dividend)
        divisor = jnp.where(later, rate * divisor + 1.0, divisor)
    inverse = divisor / dividend
    outs = rest[-1 - chips : -1]
    for q in range(chips):
        outs[q][...] = (rest[q][...] * inverse).astype(jnp.bfloat16)
    rest[-1][...] = jnp.zeros((8, LANES), jnp.int32)


def normalise(section, levels, decay, sums, scale, after):
    spec = pl.BlockSpec(memory_space=pltpu.VMEM)
    outs = pl.pallas_call(
        functools.partial(normalise_kernel, levels.shape[0], len(sums), scale),
        in_specs=[pl.BlockSpec(memory_space=pltpu.SMEM)]
        + [spec] * (2 + len(sums))
        + [pl.BlockSpec(memory_space=pl.ANY)] * len(after),
        out_specs=[spec] * (len(sums) + 1),
        out_shape=[jax.ShapeDtypeStruct(s.shape, jnp.bfloat16) for s in sums] + [TOKEN],
        compiler_params=pltpu.CompilerParams(vmem_limit_bytes=VMEM),
        cost_estimate=COST,
        name="normalise",
    )(section, levels, decay, *sums, *after)
    return outs[:-1], outs[-1]


def dedisperse_kernel(shards, size, last, first, scale, place, cosine, sine, *rest):
    total = None if first else rest[shards]
    if last:
        out, token, upper, lower, woven = rest[-5:]
    else:
        out, token, upper, lower = rest[-4:]
    token[...] = jnp.zeros((8, LANES), jnp.int32)
    f = pl.program_id(0)
    for part, m in zip(rest, slots(shards)):
        at = pl.ds(pl.multiple_of((place[0] ^ m) * size, size), size)
        real, imag = part[f], part[f + MODF]
        upper[at, :LANES] = real
        upper[at, LANES:] = imag
        lower[at, :LANES] = imag
        lower[at, LANES:] = -real
    value = jnp.dot(cosine[0], upper[...], preferred_element_type=jnp.float32) + jnp.dot(
        sine[0], lower[...], preferred_element_type=jnp.float32
    )
    if total is not None:
        value = value + total[0]
    if last:
        rows = value.shape[0]
        woven[pl.ds(0, rows, stride=2), :] = value[:, :LANES] * scale
        woven[pl.ds(1, rows, stride=2), :] = value[:, LANES:] * scale
        out[0] = woven[...].astype(out.dtype)
    else:
        out[0] = value


def dedisperse(place, cosine, sine, at, parts, total, last, scale, after):
    shards, size = len(parts), parts[0].shape[1]
    rows, depth = cosine.shape[1], shards * size
    each = lambda f, _: (f, 0, 0)
    block = (2 * MODF, size, LANES)
    sums = [] if total is None else [total]
    made = (2 * rows, LANES) if last else (rows, 2 * LANES)
    return pl.pallas_call(
        functools.partial(dedisperse_kernel, shards, size, last, total is None, scale),
        grid_spec=pltpu.PrefetchScalarGridSpec(
            num_scalar_prefetch=1,
            grid=(MODF,),
            in_specs=[pl.BlockSpec((1, rows, depth), lambda f, _: (f, 0, at // depth))] * 2
            + [pl.BlockSpec(block, lambda f, _: (0, 0, 0))] * shards
            + [pl.BlockSpec((1, rows, 2 * LANES), each)] * len(sums)
            + [pl.BlockSpec(memory_space=pl.ANY)] * len(after),
            out_specs=[pl.BlockSpec((1,) + made, each), pl.BlockSpec((8, LANES), lambda f, _: (0, 0))],
            scratch_shapes=[pltpu.VMEM((depth, 2 * LANES), jnp.bfloat16)] * 2
            + ([pltpu.VMEM(made, jnp.float32)] if last else []),
        ),
        out_shape=[jax.ShapeDtypeStruct((MODF,) + made, jnp.bfloat16 if last else jnp.float32), TOKEN],
        compiler_params=pltpu.CompilerParams(vmem_limit_bytes=24 << 20),
        cost_estimate=COST,
        name="dedisperse",
    )(place, cosine, sine, *parts, *sums, *after)


def phase_tables(delay, frames):
    turn = jnp.arange(1, MODF + 1, dtype=jnp.int32)[:, None, None] * delay[None]
    cosine = cosine_of(turn, frames).astype(jnp.bfloat16)
    sine = cosine_of(turn - frames // 4, frames).astype(jnp.bfloat16)
    return cosine, sine


def chunk_sizes(channels):
    edge, inner = ROWS, 2 * ROWS
    if channels < 2 * edge + inner:
        return [ROWS] * (channels // ROWS)
    left = channels - 2 * edge
    sizes = [edge] + [inner] * (left // inner) + ([left % inner] if left % inner else []) + [edge]
    return sizes


def pipelined(voltages, feed_gains, grid_index, decay_rates, delays):
    shards, blocks = lax.axis_size("shard"), lax.axis_size("section")
    frames = voltages.shape[3] // NSAMP
    chans, trials = delays.shape
    feeds = grid_index.shape[0]
    local = chans // shards
    place = lax.axis_index("shard").reshape(1)
    section = lax.axis_index("section").reshape(1)
    sizes = [32, 64, 32]
    starts = [sum(sizes[:c]) for c in range(len(sizes))]
    rows = spectral_constant(chans).reshape(2, shards, local, NSAMP)
    scale = np.float32(1.0 / (frames * feeds))

    def exchange(parts):
        return [
            lax.ppermute(part, "shard", [(j, j ^ m) for j in range(shards)]) if m else part
            for part, m in zip(parts, slots(shards))
        ]

    def send_spectra(c, after):
        table = np.ascontiguousarray(rows[:, :, starts[c] : starts[c] + sizes[c]].transpose(1, 0, 2, 3))
        table = jnp.asarray(table.reshape(-1, NSAMP))
        parts, token = channelize(place, table, voltages, sizes[c], shards, after)
        return exchange(parts), token

    order = sorted(range(len(sizes)), key=lambda c: -sizes[c])
    column = {c: shards * sum(sizes[e] for e in order[: order.index(c)]) for c in order}

    def make_phases(token):
        by_shard = ((delays + token[0, 0]) & (frames - 1)).reshape(shards, local, trials)
        by_chunk = [by_shard[:, starts[c] : starts[c] + sizes[c]].reshape(-1, trials) for c in order]
        return phase_tables(jnp.transpose(jnp.concatenate(by_chunk)), frames)

    count = len(sizes)
    received, modulated = {}, {}
    total, phases = None, None

    def add_chunk(c, total, after):
        last = c + 1 == count
        return dedisperse(place, *phases, column[c], modulated[c], total, last, np.float32(1.0 / math.sqrt(chans)), after)

    received[0], token = send_spectra(0, [])
    received[1], token = send_spectra(1, [token])
    table = beam_table(grid_index + token[0, 0])
    for c in range(count):
        start, size = starts[c], sizes[c]
        sums, level = form_beams(place, feed_gains, table, received[c], start, size, frames, [token])
        levels = lax.all_gather(level, "section")
        decay = decay_rates[start : start + size].reshape(size, 1)
        ready, token = normalise(section, levels, decay, sums, scale, [])
        modulated[c] = exchange(ready)
        if c == 0:
            phases = make_phases(token)
            token = phases[0]
        else:
            total, token = add_chunk(c - 1, total, [token])
        if c + 2 < count:
            received[c + 2], token = send_spectra(c + 2, [token])
    total, _ = add_chunk(count - 1, total, [])
    return total.reshape(1, MODF, trials, 2, feeds // shards)


def plain(voltages, feed_gains, grid_index, decay_rates, delays):
    shards = lax.axis_size("shard")
    chans, trials = delays.shape
    feeds, local_feeds = grid_index.shape[0], voltages.shape[2]
    frames = voltages.shape[3] // NSAMP
    samples = voltages[0].reshape(POL * local_feeds * frames, NSAMP)
    rows = jnp.asarray(spectral_constant(chans).reshape(2 * chans, NSAMP))
    spectra = lax.dot_general(rows, samples, (((1,), (1,)), ((), ())), preferred_element_type=jnp.float32)
    spectra = (spectra * (1.0 / math.sqrt(NSAMP))).astype(jnp.bfloat16)
    spectra = spectra.reshape(2, chans, POL, local_feeds, frames)
    turned = lax.all_to_all(spectra, "shard", split_axis=1, concat_axis=3, tiled=True)
    values = turned.astype(jnp.float32)
    gain = feed_gains.astype(jnp.float32)[:, :, None, :, None]
    calibrated = jnp.stack(
        [gain[0] * values[0] - gain[1] * values[1], gain[0] * values[1] + gain[1] * values[0]]
    ).astype(jnp.bfloat16)
    table = beam_table(grid_index).reshape(2, feeds, feeds // LANES, 2, LANES)
    beams = jnp.einsum("akpfn,afdel->eknpdl", calibrated, table, preferred_element_type=jnp.float32)
    power = jnp.sum(beams * beams, axis=(0, 3)).reshape(-1, frames, feeds)
    levels = jnp.mean(power, axis=(1, 2)) + 1e-06
    gathered = lax.all_gather(levels, "section")
    dividend, divisor = jnp.zeros_like(levels), jnp.zeros_like(levels)
    for block in range(gathered.shape[0]):
        later = block <= lax.axis_index("section")
        dividend = jnp.where(later, decay_rates * dividend + gathered[block], dividend)
        divisor = jnp.where(later, decay_rates * divisor + 1.0, divisor)
    power = power * (divisor / dividend)[:, None, None]
    sums = jnp.stack(frame_sums([power[:, n] for n in range(frames)])).astype(jnp.bfloat16)
    moved = lax.all_to_all(sums, "shard", split_axis=2, concat_axis=1, tiled=True)
    turn = jnp.arange(1, MODF + 1, dtype=jnp.int32)[:, None, None] * (delays & (frames - 1))[None]
    cosine = cosine_of(turn, frames).astype(jnp.bfloat16)
    sine = cosine_of(turn - frames // 4, frames).astype(jnp.bfloat16)
    dot = functools.partial(jnp.einsum, "fkt,fkb->ftb", preferred_element_type=jnp.float32)
    real, imag = moved[:MODF], moved[MODF:]
    result = jnp.stack(
        [dot(cosine, real) + dot(sine, imag), dot(cosine, imag) - dot(sine, real)], 2
    ) * (1.0 / math.sqrt(chans))
    return result.astype(jnp.bfloat16)[None]


def solution(mesh):
    def shards(voltages, feed_gains, grid_index, decay_rates, delays):
        count = lax.axis_size("shard")
        fits = (
            voltages.shape[2] == LANES
            and grid_index.shape[0] == count * LANES
            and delays.shape[0] % (count * ROWS) == 0
            and voltages.shape[3] == ROWS * NSAMP
            and count & (count - 1) == 0
            and delays.shape[0] // count >= 2 * ROWS
        )
        form = pipelined if fits else plain
        return form(voltages, feed_gains, grid_index, decay_rates, delays)

    in_specs = (P("section", None, "shard", None), P(None, "shard", None), P(), P("shard"), P())
    out_specs = P("section", None, None, None, "shard")
    return jax.shard_map(shards, mesh=mesh, in_specs=in_specs, out_specs=out_specs, check_vma=False)
```

```python
import functools
import math

import jax
import jax.numpy as jnp
import numpy as np
from jax import lax
from jax.experimental import pallas as pl
from jax.experimental.pallas import tpu as pltpu
from jax.sharding import PartitionSpec as P

POL = 2
GRID_X = 4
GRID_Y = 256
NSAMP = 2048
MODF = 7
LANES = 128
ROWS = 16
COST = pl.CostEstimate(flops=1000, bytes_accessed=1000, transcendentals=0)
TOKEN = jax.ShapeDtypeStruct((8, LANES), jnp.int32)
VMEM = 60 << 20


def spectral_constant(chans):
    row_index = np.arange(chans, dtype=np.int64)[:, None]
    col_index = np.arange(NSAMP, dtype=np.int64)[None, :]
    angles = np.float32(2.0 * math.pi / NSAMP) * (row_index * col_index % NSAMP).astype(np.float32)
    return np.stack([np.cos(angles), -np.sin(angles)], 0).astype(np.float32).astype(jnp.bfloat16)


def cosine_of(index, period):
    half, quarter = period // 2, period // 4
    folded = jnp.abs(((index + half) & (period - 1)) - half) - quarter
    x = folded.astype(jnp.float32) * np.float32(2.0 * math.pi / period)
    x2 = x * x
    series = np.float32(-1.0 / math.factorial(11))
    for order in (9, 7, 5, 3, 1):
        sign = 1.0 if order % 4 == 1 else -1.0
        series = series * x2 + np.float32(sign / math.factorial(order))
    return -x * series


def beam_table(grid_index):
    feeds = grid_index.shape[0]
    cell = jnp.concatenate([grid_index, grid_index])[:, None]
    part = lax.broadcasted_iota(jnp.int32, (2 * feeds, 1), 0) // feeds
    column = lax.broadcasted_iota(jnp.int32, (1, 2 * feeds), 1)
    end = (column // LANES) % 2
    beam = column // (2 * LANES) * LANES + column % LANES
    x, y = cell // GRID_Y, cell % GRID_Y
    u, w = beam // GRID_Y, beam % GRID_Y
    turn = y * w + (GRID_Y // GRID_X) * (x * u) + (GRID_Y // 4) * (end - part)
    return cosine_of(turn, GRID_Y).astype(jnp.bfloat16)


def frame_sums(frames):
    even = [frames[n] + frames[n + 8] for n in range(8)]
    odd = [frames[n] - frames[n + 8] for n in range(8)]
    ee = [even[n] + even[n + 4] for n in range(4)]
    ed = [even[n] - even[n + 4] for n in range(4)]
    real, imag = [None] * 8, [None] * 8
    real[4] = ee[0] - ee[2]
    imag[4] = ee[3] - ee[1]
    root = np.float32(math.sqrt(0.5))
    diff, total = root * (ed[1] - ed[3]), root * (ed[1] + ed[3])
    real[2], imag[2] = ed[0] + diff, -ed[2] - total
    real[6], imag[6] = ed[0] - diff, ed[2] - total
    minus = [None] + [odd[n] - odd[8 - n] for n in (1, 2, 3)]
    plus = [None] + [odd[n] + odd[8 - n] for n in (1, 2, 3)]
    for f in (1, 3, 5, 7):
        c = [np.float32(math.cos(math.pi * f * n / 8)) for n in range(4)]
        s = [np.float32(math.sin(math.pi * f * n / 8)) for n in range(5)]
        real[f] = odd[0] + (c[1] * minus[1] + c[2] * minus[2] + c[3] * minus[3])
        last = odd[4] if s[4] > 0 else -odd[4]
        imag[f] = -(last + (s[1] * plus[1] + s[2] * plus[2] + s[3] * plus[3]))
    return [np.float32(0.25) * v for v in real[1:] + imag[1:]]


def slots(shards):
    return [m for m in range(shards // 2, shards)] + [m for m in range(shards // 2 - 1, -1, -1)]


def channelize_kernel(shards, size, frames, n_after, place, table, volts, *rest):
    outs, zero, held = rest[n_after : n_after + shards], rest[-2], rest[-1]
    zero[...] = jnp.zeros((8, LANES), jnp.int32)
    for n in range(frames):
        samples = volts[0, :, :, n * NSAMP : (n + 1) * NSAMP].reshape(-1, NSAMP)
        product = lax.dot_general(
            table[...], samples, (((1,), (1,)), ((), ())), preferred_element_type=jnp.float32
        )
        held[...] = (product * np.float32(1.0 / math.sqrt(NSAMP))).reshape(held.shape)
        for out, m in zip(outs, slots(shards)):
            mine = held[place[0] ^ m].astype(jnp.bfloat16)
            for a in range(2):
                for p in range(POL):
                    out[a, p, n] = mine[a * size : (a + 1) * size, p * LANES : (p + 1) * LANES]


def channelize(place, table, voltages, size, shards, after):
    total = voltages.shape[3] // NSAMP
    frames = 2 if size < 32 else 4
    shape = (2, POL, total, size, LANES)
    block = (2, POL, frames, size, LANES)
    outs = pl.pallas_call(
        functools.partial(channelize_kernel, shards, size, frames, len(after)),
        grid_spec=pltpu.PrefetchScalarGridSpec(
            num_scalar_prefetch=1,
            grid=(total // frames,),
            in_specs=[
                pl.BlockSpec(table.shape, lambda n, _: (0, 0)),
                pl.BlockSpec((1, POL, LANES, frames * NSAMP), lambda n, _: (0, 0, 0, n)),
            ]
            + [pl.BlockSpec(memory_space=pl.ANY)] * len(after),
            out_specs=[pl.BlockSpec(block, lambda n, _: (0, 0, n, 0, 0))] * shards
            + [pl.BlockSpec((8, LANES), lambda n, _: (0, 0))],
            scratch_shapes=[pltpu.VMEM((shards, 2 * size, POL * LANES), jnp.float32)],
        ),
        out_shape=[jax.ShapeDtypeStruct(shape, jnp.bfloat16)] * shards
        + [jax.ShapeDtypeStruct((8, LANES), jnp.int32)],
        compiler_params=pltpu.CompilerParams(vmem_limit_bytes=VMEM),
        cost_estimate=COST,
        name="channelize",
    )(place, table, voltages, *after)
    return outs[:-1], outs[-1]


def beam_kernel(shards, frames, place, gains, table, *rest):
    outs, level, held = rest[-2 - shards : -2], rest[-2], rest[-1]
    feeds = shards * LANES
    rows = POL * frames * ROWS
    for spectra, m in zip(rest, slots(shards)):
        at = pl.multiple_of((place[0] ^ m) * LANES, LANES)
        gain_real = gains[0, :, pl.ds(at, LANES)].astype(jnp.float32)
        gain_imag = gains[1, :, pl.ds(at, LANES)].astype(jnp.float32)
        real = spectra[0].astype(jnp.float32)
        imag = spectra[1].astype(jnp.float32)
        cal_real = (gain_real * real - gain_imag * imag).astype(jnp.bfloat16)
        cal_imag = (gain_real * imag + gain_imag * real).astype(jnp.bfloat16)
        held[:, pl.ds(at, LANES)] = cal_real.reshape(rows, LANES)
        held[:, pl.ds(pl.multiple_of(at + feeds, LANES), LANES)] = cal_imag.reshape(rows, LANES)
    sums = jnp.zeros((ROWS, LANES), jnp.float32)
    for out, m in zip(outs, slots(shards)):
        at = pl.multiple_of((place[0] ^ m) * (2 * LANES), 2 * LANES)
        beams = jnp.dot(held[...], table[:, pl.ds(at, 2 * LANES)], preferred_element_type=jnp.float32)
        squares = beams * beams
        power = squares[:, :LANES] + squares[:, LANES:]
        power = (power[: rows // 2] + power[rows // 2 :]).reshape(frames, ROWS, LANES)
        sums = sums + jnp.sum(power, axis=0)
        for q, value in enumerate(frame_sums(power)):
            out[q] = value
    level[...] = sums


def form_beams(place, gains, table, spectra, start, size, frames, after):
    shards = len(spectra)
    block = (2, POL, frames, ROWS, LANES)
    outs = pl.pallas_call(
        functools.partial(beam_kernel, shards, frames),
        grid_spec=pltpu.PrefetchScalarGridSpec(
            num_scalar_prefetch=1,
            grid=(size // ROWS,),
            in_specs=[
                pl.BlockSpec((2, ROWS, gains.shape[2]), lambda g, _: (0, start // ROWS + g, 0)),
                pl.BlockSpec(table.shape, lambda g, _: (0, 0), pipeline_mode=pl.Buffered(1)),
            ]
            + [pl.BlockSpec(block, lambda g, _: (0, 0, 0, g, 0))] * shards
            + [pl.BlockSpec(memory_space=pl.ANY)] * len(after),
            out_specs=[pl.BlockSpec((2 * MODF, ROWS, LANES), lambda g, _: (0, g, 0))] * shards
            + [pl.BlockSpec((ROWS, LANES), lambda g, _: (g, 0))],
            scratch_shapes=[pltpu.VMEM((POL * frames * ROWS, table.shape[0]), jnp.bfloat16)],
        ),
        out_shape=[jax.ShapeDtypeStruct((2 * MODF, size, LANES), jnp.float32)] * shards
        + [jax.ShapeDtypeStruct((size, LANES), jnp.float32)],
        compiler_params=pltpu.CompilerParams(vmem_limit_bytes=VMEM),
        cost_estimate=COST,
        name="form_beams",
    )(place, gains, table, *spectra, *after)
    return outs[:-1], outs[-1]


def normalise_kernel(count, shards, scale, section, levels, decay, *rest):
    rate = decay[...]
    dividend, divisor = jnp.zeros_like(rate), jnp.zeros_like(rate)
    for block in range(count):
        mean = jnp.sum(levels[block], axis=1, keepdims=True) * scale + np.float32(1e-6)
        later = block <= section[0]
        dividend = jnp.where(later, rate * dividend + mean, dividend)
        divisor = jnp.where(later, rate * divisor + 1.0, divisor)
    inverse = divisor / dividend
    outs = rest[-1 - shards : -1]
    for m in range(shards):
        outs[m][...] = (rest[m][...] * inverse).astype(jnp.bfloat16)
    rest[-1][...] = jnp.zeros((8, LANES), jnp.int32)


def normalise(section, levels, decay, sums, scale, after):
    spec = pl.BlockSpec(memory_space=pltpu.VMEM)
    outs = pl.pallas_call(
        functools.partial(normalise_kernel, levels.shape[0], len(sums), scale),
        in_specs=[pl.BlockSpec(memory_space=pltpu.SMEM)]
        + [spec] * (2 + len(sums))
        + [pl.BlockSpec(memory_space=pl.ANY)] * len(after),
        out_specs=[spec] * (len(sums) + 1),
        out_shape=[jax.ShapeDtypeStruct(s.shape, jnp.bfloat16) for s in sums] + [TOKEN],
        compiler_params=pltpu.CompilerParams(vmem_limit_bytes=VMEM),
        cost_estimate=COST,
        name="normalise",
    )(section, levels, decay, *sums, *after)
    return outs[:-1], outs[-1]


def dedisperse_kernel(shards, columns, sizes, scale, place, cosine, sine, *rest):
    out, upper, lower, woven = rest[-4:]
    f = pl.program_id(0)
    for c, (column, size) in enumerate(zip(columns, sizes)):
        for part, m in zip(rest[c * shards : (c + 1) * shards], slots(shards)):
            at = pl.ds(pl.multiple_of(column + (place[0] ^ m) * size, ROWS), size)
            real, imag = part[f], part[f + MODF]
            upper[at, :LANES] = real
            upper[at, LANES:] = imag
            lower[at, :LANES] = imag
            lower[at, LANES:] = -real
    value = jnp.dot(cosine[0], upper[...], preferred_element_type=jnp.float32) + jnp.dot(
        sine[0], lower[...], preferred_element_type=jnp.float32
    )
    rows = value.shape[0]
    woven[pl.ds(0, rows, stride=2), :] = value[:, :LANES] * scale
    woven[pl.ds(1, rows, stride=2), :] = value[:, LANES:] * scale
    out[0] = woven[...].astype(out.dtype)


def dedisperse(place, cosine, sine, columns, chunks, scale):
    shards = len(chunks[0])
    sizes = [parts[0].shape[1] for parts in chunks]
    rows, depth = cosine.shape[1:]
    each = lambda f, _: (f, 0, 0)
    made = (2 * rows, LANES)
    return pl.pallas_call(
        functools.partial(dedisperse_kernel, shards, columns, sizes, scale),
        grid_spec=pltpu.PrefetchScalarGridSpec(
            num_scalar_prefetch=1,
            grid=(MODF,),
            in_specs=[pl.BlockSpec((1, rows, depth), each)] * 2
            + [pl.BlockSpec((2 * MODF, size, LANES), lambda f, _: (0, 0, 0)) for size in sizes for _ in range(shards)],
            out_specs=pl.BlockSpec((1,) + made, each),
            scratch_shapes=[pltpu.VMEM((depth, 2 * LANES), jnp.bfloat16)] * 2 + [pltpu.VMEM(made, jnp.float32)],
        ),
        out_shape=jax.ShapeDtypeStruct((MODF,) + made, jnp.bfloat16),
        compiler_params=pltpu.CompilerParams(vmem_limit_bytes=60 << 20),
        cost_estimate=COST,
        name="dedisperse",
    )(place, cosine, sine, *[part for parts in chunks for part in parts])


def phase_tables(delay, frames):
    turn = jnp.arange(1, MODF + 1, dtype=jnp.int32)[:, None, None] * delay[None]
    cosine = cosine_of(turn, frames).astype(jnp.bfloat16)
    sine = cosine_of(turn - frames // 4, frames).astype(jnp.bfloat16)
    return cosine, sine


def chunk_sizes(channels):
    edge, inner = ROWS, 2 * ROWS
    if channels < 2 * edge + inner:
        return [ROWS] * (channels // ROWS)
    left = channels - 2 * edge
    sizes = [edge] + [inner] * (left // inner) + ([left % inner] if left % inner else []) + [edge]
    return sizes


def pipelined(voltages, feed_gains, grid_index, decay_rates, delays):
    shards, blocks = lax.axis_size("shard"), lax.axis_size("section")
    frames = voltages.shape[3] // NSAMP
    chans, trials = delays.shape
    feeds = grid_index.shape[0]
    local = chans // shards
    place = lax.axis_index("shard").reshape(1)
    section = lax.axis_index("section").reshape(1)
    sizes = [32, 64, 32]
    starts = [sum(sizes[:c]) for c in range(len(sizes))]
    rows = spectral_constant(chans).reshape(2, shards, local, NSAMP)
    scale = np.float32(1.0 / (frames * feeds))

    far, near = slots(shards)[: shards // 2], slots(shards)[shards // 2 :]

    def exchange(parts, partners):
        return [
            lax.ppermute(part, "shard", [(j, j ^ m) for j in range(shards)]) if m else part
            for part, m in zip(parts, partners)
        ]

    def send_spectra(c, after):
        table = np.ascontiguousarray(rows[:, :, starts[c] : starts[c] + sizes[c]].transpose(1, 0, 2, 3))
        table = jnp.asarray(table.reshape(-1, NSAMP))
        parts, token = channelize(place, table, voltages, sizes[c], shards, after)
        return exchange(parts, far + near), token

    columns = [shards * at for at in starts]

    def make_phases(token):
        by_shard = ((delays + token[0, 0]) & (frames - 1)).reshape(shards, local, trials)
        by_chunk = [by_shard[:, at : at + size].reshape(-1, trials) for at, size in zip(starts, sizes)]
        return phase_tables(jnp.transpose(jnp.concatenate(by_chunk)), frames)

    count = len(sizes)
    received, modulated = {}, {}
    phases = None

    received[0], token = send_spectra(0, [])
    received[1], token = send_spectra(1, [token])
    table = beam_table(grid_index + token[0, 0])
    half, late = shards // 2, []
    for c in range(count):
        start, size = starts[c], sizes[c]
        last = c + 1 == count
        ahead = modulated[c - 1] if 0 < c < count - 1 else []
        sums, level = form_beams(place, feed_gains, table, received[c], start, size, frames, [token] + ahead)
        levels = lax.all_gather(level, "section")
        decay = decay_rates[start : start + size].reshape(size, 1)
        if not last:
            ready, token = normalise(section, levels, decay, sums[:half], scale, [])
            modulated[c] = exchange(ready, far)
            late.append((c, (levels, decay, sums[half:])))
        else:
            after = modulated[c - 1][:half] if c else []
            ready, token = normalise(section, levels, decay, sums, scale, after)
            modulated[c] = exchange(ready, far + near)
        if last:
            for e, held in late:
                modulated[e] = modulated[e] + exchange(normalise(section, *held, scale, [token])[0], near)
        if c == 0:
            phases = make_phases(token)
            token = phases[0]
        if c + 2 < count:
            received[c + 2], token = send_spectra(c + 2, [token])
    chunks = [modulated[c] for c in reversed(range(count))]
    total = dedisperse(place, *phases, columns[::-1], chunks, np.float32(1.0 / math.sqrt(chans)))
    return total.reshape(1, MODF, trials, 2, feeds // shards)


def plain(voltages, feed_gains, grid_index, decay_rates, delays):
    shards = lax.axis_size("shard")
    chans, trials = delays.shape
    feeds, local_feeds = grid_index.shape[0], voltages.shape[2]
    frames = voltages.shape[3] // NSAMP
    samples = voltages[0].reshape(POL * local_feeds * frames, NSAMP)
    rows = jnp.asarray(spectral_constant(chans).reshape(2 * chans, NSAMP))
    spectra = lax.dot_general(rows, samples, (((1,), (1,)), ((), ())), preferred_element_type=jnp.float32)
    spectra = (spectra * (1.0 / math.sqrt(NSAMP))).astype(jnp.bfloat16)
    spectra = spectra.reshape(2, chans, POL, local_feeds, frames)
    turned = lax.all_to_all(spectra, "shard", split_axis=1, concat_axis=3, tiled=True)
    values = turned.astype(jnp.float32)
    gain = feed_gains.astype(jnp.float32)[:, :, None, :, None]
    calibrated = jnp.stack(
        [gain[0] * values[0] - gain[1] * values[1], gain[0] * values[1] + gain[1] * values[0]]
    ).astype(jnp.bfloat16)
    table = beam_table(grid_index).reshape(2, feeds, feeds // LANES, 2, LANES)
    beams = jnp.einsum("akpfn,afdel->eknpdl", calibrated, table, preferred_element_type=jnp.float32)
    power = jnp.sum(beams * beams, axis=(0, 3)).reshape(-1, frames, feeds)
    levels = jnp.mean(power, axis=(1, 2)) + 1e-06
    gathered = lax.all_gather(levels, "section")
    dividend, divisor = jnp.zeros_like(levels), jnp.zeros_like(levels)
    for block in range(gathered.shape[0]):
        later = block <= lax.axis_index("section")
        dividend = jnp.where(later, decay_rates * dividend + gathered[block], dividend)
        divisor = jnp.where(later, decay_rates * divisor + 1.0, divisor)
    power = power * (divisor / dividend)[:, None, None]
    sums = jnp.stack(frame_sums([power[:, n] for n in range(frames)])).astype(jnp.bfloat16)
    moved = lax.all_to_all(sums, "shard", split_axis=2, concat_axis=1, tiled=True)
    turn = jnp.arange(1, MODF + 1, dtype=jnp.int32)[:, None, None] * (delays & (frames - 1))[None]
    cosine = cosine_of(turn, frames).astype(jnp.bfloat16)
    sine = cosine_of(turn - frames // 4, frames).astype(jnp.bfloat16)
    dot = functools.partial(jnp.einsum, "fkt,fkb->ftb", preferred_element_type=jnp.float32)
    real, imag = moved[:MODF], moved[MODF:]
    result = jnp.stack(
        [dot(cosine, real) + dot(sine, imag), dot(cosine, imag) - dot(sine, real)], 2
    ) * (1.0 / math.sqrt(chans))
    return result.astype(jnp.bfloat16)[None]


def solution(mesh):
    def shards(voltages, feed_gains, grid_index, decay_rates, delays):
        count = lax.axis_size("shard")
        fits = (
            voltages.shape[2] == LANES
            and grid_index.shape[0] == count * LANES
            and delays.shape[0] % (count * ROWS) == 0
            and voltages.shape[3] == ROWS * NSAMP
            and count & (count - 1) == 0
            and delays.shape[0] // count >= 2 * ROWS
        )
        form = pipelined if fits else plain
        return form(voltages, feed_gains, grid_index, decay_rates, delays)

    in_specs = (P("section", None, "shard", None), P(None, "shard", None), P(), P("shard"), P())
    out_specs = P("section", None, None, None, "shard")
    return jax.shard_map(shards, mesh=mesh, in_specs=in_specs, out_specs=out_specs, check_vma=False)
```

```python
import functools
import math

import jax
import jax.numpy as jnp
import numpy as np
from jax import lax
from jax.experimental import pallas as pl
from jax.experimental.pallas import tpu as pltpu
from jax.sharding import PartitionSpec as P

POL = 2
GRID_X = 4
GRID_Y = 256
NSAMP = 2048
MODF = 7
LANES = 128
ROWS = 16
COST = pl.CostEstimate(flops=1000, bytes_accessed=1000, transcendentals=0)
TOKEN = jax.ShapeDtypeStruct((8, LANES), jnp.int32)
VMEM = 60 << 20


def spectral_constant(chans):
    row_index = np.arange(chans, dtype=np.int64)[:, None]
    col_index = np.arange(NSAMP, dtype=np.int64)[None, :]
    angles = np.float32(2.0 * math.pi / NSAMP) * (row_index * col_index % NSAMP).astype(np.float32)
    return np.stack([np.cos(angles), -np.sin(angles)], 0).astype(np.float32).astype(jnp.bfloat16)


def cosine_of(index, period):
    half, quarter = period // 2, period // 4
    folded = jnp.abs(((index + half) & (period - 1)) - half) - quarter
    x = folded.astype(jnp.float32) * np.float32(2.0 * math.pi / period)
    x2 = x * x
    series = np.float32(-1.0 / math.factorial(11))
    for order in (9, 7, 5, 3, 1):
        sign = 1.0 if order % 4 == 1 else -1.0
        series = series * x2 + np.float32(sign / math.factorial(order))
    return -x * series


def beam_table(grid_index):
    feeds = grid_index.shape[0]
    cell = jnp.concatenate([grid_index, grid_index])[:, None]
    part = lax.broadcasted_iota(jnp.int32, (2 * feeds, 1), 0) // feeds
    column = lax.broadcasted_iota(jnp.int32, (1, 2 * feeds), 1)
    end = (column // LANES) % 2
    beam = column // (2 * LANES) * LANES + column % LANES
    x, y = cell // GRID_Y, cell % GRID_Y
    u, w = beam // GRID_Y, beam % GRID_Y
    turn = y * w + (GRID_Y // GRID_X) * (x * u) + (GRID_Y // 4) * (end - part)
    return cosine_of(turn, GRID_Y).astype(jnp.bfloat16)


def frame_sums(frames):
    even = [frames[n] + frames[n + 8] for n in range(8)]
    odd = [frames[n] - frames[n + 8] for n in range(8)]
    ee = [even[n] + even[n + 4] for n in range(4)]
    ed = [even[n] - even[n + 4] for n in range(4)]
    real, imag = [None] * 8, [None] * 8
    real[4] = ee[0] - ee[2]
    imag[4] = ee[3] - ee[1]
    root = np.float32(math.sqrt(0.5))
    diff, total = root * (ed[1] - ed[3]), root * (ed[1] + ed[3])
    real[2], imag[2] = ed[0] + diff, -ed[2] - total
    real[6], imag[6] = ed[0] - diff, ed[2] - total
    minus = [None] + [odd[n] - odd[8 - n] for n in (1, 2, 3)]
    plus = [None] + [odd[n] + odd[8 - n] for n in (1, 2, 3)]
    for f in (1, 3, 5, 7):
        c = [np.float32(math.cos(math.pi * f * n / 8)) for n in range(4)]
        s = [np.float32(math.sin(math.pi * f * n / 8)) for n in range(5)]
        real[f] = odd[0] + (c[1] * minus[1] + c[2] * minus[2] + c[3] * minus[3])
        last = odd[4] if s[4] > 0 else -odd[4]
        imag[f] = -(last + (s[1] * plus[1] + s[2] * plus[2] + s[3] * plus[3]))
    return [np.float32(0.25) * v for v in real[1:] + imag[1:]]


def slots(shards):
    return [m for m in range(shards // 2, shards)] + [m for m in range(shards // 2 - 1, -1, -1)]


def channelize_kernel(shards, size, frames, n_after, place, table, volts, *rest):
    outs, zero, held = rest[n_after : n_after + shards], rest[-2], rest[-1]
    zero[...] = jnp.zeros((8, LANES), jnp.int32)
    for n in range(frames):
        samples = volts[0, :, :, n * NSAMP : (n + 1) * NSAMP].reshape(-1, NSAMP)
        product = lax.dot_general(
            table[...], samples, (((1,), (1,)), ((), ())), preferred_element_type=jnp.float32
        )
        held[...] = (product * np.float32(1.0 / math.sqrt(NSAMP))).reshape(held.shape)
        for out, m in zip(outs, slots(shards)):
            mine = held[place[0] ^ m].astype(jnp.bfloat16)
            for a in range(2):
                for p in range(POL):
                    out[a, p, n] = mine[a * size : (a + 1) * size, p * LANES : (p + 1) * LANES]


def channelize(place, table, voltages, size, shards, after):
    total = voltages.shape[3] // NSAMP
    frames = 2 if size < 32 else 4
    shape = (2, POL, total, size, LANES)
    block = (2, POL, frames, size, LANES)
    outs = pl.pallas_call(
        functools.partial(channelize_kernel, shards, size, frames, len(after)),
        grid_spec=pltpu.PrefetchScalarGridSpec(
            num_scalar_prefetch=1,
            grid=(total // frames,),
            in_specs=[
                pl.BlockSpec(table.shape, lambda n, _: (0, 0)),
                pl.BlockSpec((1, POL, LANES, frames * NSAMP), lambda n, _: (0, 0, 0, n)),
            ]
            + [pl.BlockSpec(memory_space=pl.ANY)] * len(after),
            out_specs=[pl.BlockSpec(block, lambda n, _: (0, 0, n, 0, 0))] * shards
            + [pl.BlockSpec((8, LANES), lambda n, _: (0, 0))],
            scratch_shapes=[pltpu.VMEM((shards, 2 * size, POL * LANES), jnp.float32)],
        ),
        out_shape=[jax.ShapeDtypeStruct(shape, jnp.bfloat16)] * shards
        + [jax.ShapeDtypeStruct((8, LANES), jnp.int32)],
        compiler_params=pltpu.CompilerParams(vmem_limit_bytes=VMEM),
        cost_estimate=COST,
        name="channelize",
    )(place, table, voltages, *after)
    return outs[:-1], outs[-1]


def beam_kernel(shards, frames, place, gains, table, *rest):
    outs, level, held = rest[-2 - shards : -2], rest[-2], rest[-1]
    feeds = shards * LANES
    rows = POL * frames * ROWS
    for spectra, m in zip(rest, slots(shards)):
        at = pl.multiple_of((place[0] ^ m) * LANES, LANES)
        gain_real = gains[0, :, pl.ds(at, LANES)].astype(jnp.float32)
        gain_imag = gains[1, :, pl.ds(at, LANES)].astype(jnp.float32)
        real = spectra[0].astype(jnp.float32)
        imag = spectra[1].astype(jnp.float32)
        cal_real = (gain_real * real - gain_imag * imag).astype(jnp.bfloat16)
        cal_imag = (gain_real * imag + gain_imag * real).astype(jnp.bfloat16)
        held[:, pl.ds(at, LANES)] = cal_real.reshape(rows, LANES)
        held[:, pl.ds(pl.multiple_of(at + feeds, LANES), LANES)] = cal_imag.reshape(rows, LANES)
    sums = jnp.zeros((ROWS, LANES), jnp.float32)
    for out, m in zip(outs, slots(shards)):
        at = pl.multiple_of((place[0] ^ m) * (2 * LANES), 2 * LANES)
        beams = jnp.dot(held[...], table[:, pl.ds(at, 2 * LANES)], preferred_element_type=jnp.float32)
        squares = beams * beams
        power = squares[:, :LANES] + squares[:, LANES:]
        power = (power[: rows // 2] + power[rows // 2 :]).reshape(frames, ROWS, LANES)
        sums = sums + jnp.sum(power, axis=0)
        for q, value in enumerate(frame_sums(power)):
            out[q] = value
    level[...] = sums


def form_beams(place, gains, table, spectra, start, size, frames, after):
    shards = len(spectra)
    block = (2, POL, frames, ROWS, LANES)
    outs = pl.pallas_call(
        functools.partial(beam_kernel, shards, frames),
        grid_spec=pltpu.PrefetchScalarGridSpec(
            num_scalar_prefetch=1,
            grid=(size // ROWS,),
            in_specs=[
                pl.BlockSpec((2, ROWS, gains.shape[2]), lambda g, _: (0, start // ROWS + g, 0)),
                pl.BlockSpec(table.shape, lambda g, _: (0, 0), pipeline_mode=pl.Buffered(1)),
            ]
            + [pl.BlockSpec(block, lambda g, _: (0, 0, 0, g, 0))] * shards
            + [pl.BlockSpec(memory_space=pl.ANY)] * len(after),
            out_specs=[pl.BlockSpec((2 * MODF, ROWS, LANES), lambda g, _: (0, g, 0))] * shards
            + [pl.BlockSpec((ROWS, LANES), lambda g, _: (g, 0))],
            scratch_shapes=[pltpu.VMEM((POL * frames * ROWS, table.shape[0]), jnp.bfloat16)],
        ),
        out_shape=[jax.ShapeDtypeStruct((2 * MODF, size, LANES), jnp.float32)] * shards
        + [jax.ShapeDtypeStruct((size, LANES), jnp.float32)],
        compiler_params=pltpu.CompilerParams(vmem_limit_bytes=VMEM),
        cost_estimate=COST,
        name="form_beams",
    )(place, gains, table, *spectra, *after)
    return outs[:-1], outs[-1]


def normalise_kernel(count, shards, scale, section, levels, decay, *rest):
    rate = decay[...]
    dividend, divisor = jnp.zeros_like(rate), jnp.zeros_like(rate)
    for block in range(count):
        mean = jnp.sum(levels[block], axis=1, keepdims=True) * scale + np.float32(1e-6)
        later = block <= section[0]
        dividend = jnp.where(later, rate * dividend + mean, dividend)
        divisor = jnp.where(later, rate * divisor + 1.0, divisor)
    inverse = divisor / dividend
    outs = rest[-1 - shards : -1]
    for m in range(shards):
        outs[m][...] = (rest[m][...] * inverse).astype(jnp.bfloat16)
    rest[-1][...] = jnp.zeros((8, LANES), jnp.int32)


def normalise(section, levels, decay, sums, scale, after):
    spec = pl.BlockSpec(memory_space=pltpu.VMEM)
    outs = pl.pallas_call(
        functools.partial(normalise_kernel, levels.shape[0], len(sums), scale),
        in_specs=[pl.BlockSpec(memory_space=pltpu.SMEM)]
        + [spec] * (2 + len(sums))
        + [pl.BlockSpec(memory_space=pl.ANY)] * len(after),
        out_specs=[spec] * (len(sums) + 1),
        out_shape=[jax.ShapeDtypeStruct(s.shape, jnp.bfloat16) for s in sums] + [TOKEN],
        compiler_params=pltpu.CompilerParams(vmem_limit_bytes=VMEM),
        cost_estimate=COST,
        name="normalise",
    )(section, levels, decay, *sums, *after)
    return outs[:-1], outs[-1]


def dedisperse_kernel(shards, columns, sizes, scale, place, cosine, sine, *rest):
    out, held, woven = rest[-3:]
    f = pl.program_id(0)
    for c, (column, size) in enumerate(zip(columns, sizes)):
        for part, m in zip(rest[c * shards : (c + 1) * shards], slots(shards)):
            at = pl.ds(pl.multiple_of(column + (place[0] ^ m) * size, ROWS), size)
            held[at, :LANES] = part[f]
            held[at, LANES:] = part[f + MODF]
    by_cosine = jnp.dot(cosine[0], held[...], preferred_element_type=jnp.float32)
    by_sine = jnp.dot(sine[0], held[...], preferred_element_type=jnp.float32)
    rows = by_cosine.shape[0]
    woven[pl.ds(0, rows, stride=2), :] = (by_cosine[:, :LANES] + by_sine[:, LANES:]) * scale
    woven[pl.ds(1, rows, stride=2), :] = (by_cosine[:, LANES:] - by_sine[:, :LANES]) * scale
    out[0] = woven[...].astype(out.dtype)


def dedisperse(place, cosine, sine, columns, chunks, scale):
    shards = len(chunks[0])
    sizes = [parts[0].shape[1] for parts in chunks]
    rows, depth = cosine.shape[1:]
    each = lambda f, _: (f, 0, 0)
    made = (2 * rows, LANES)
    return pl.pallas_call(
        functools.partial(dedisperse_kernel, shards, columns, sizes, scale),
        grid_spec=pltpu.PrefetchScalarGridSpec(
            num_scalar_prefetch=1,
            grid=(MODF,),
            in_specs=[pl.BlockSpec((1, rows, depth), each)] * 2
            + [pl.BlockSpec((2 * MODF, size, LANES), lambda f, _: (0, 0, 0)) for size in sizes for _ in range(shards)],
            out_specs=pl.BlockSpec((1,) + made, each),
            scratch_shapes=[pltpu.VMEM((depth, 2 * LANES), jnp.bfloat16), pltpu.VMEM(made, jnp.float32)],
        ),
        out_shape=jax.ShapeDtypeStruct((MODF,) + made, jnp.bfloat16),
        compiler_params=pltpu.CompilerParams(vmem_limit_bytes=60 << 20),
        cost_estimate=COST,
        name="dedisperse",
    )(place, cosine, sine, *[part for parts in chunks for part in parts])


def phase_tables(delay, frames):
    turn = jnp.arange(1, MODF + 1, dtype=jnp.int32)[:, None, None] * delay[None]
    cosine = cosine_of(turn, frames).astype(jnp.bfloat16)
    sine = cosine_of(turn - frames // 4, frames).astype(jnp.bfloat16)
    return cosine, sine


def chunk_sizes(channels):
    edge, inner = ROWS, 2 * ROWS
    if channels < 2 * edge + inner:
        return [ROWS] * (channels // ROWS)
    left = channels - 2 * edge
    sizes = [edge] + [inner] * (left // inner) + ([left % inner] if left % inner else []) + [edge]
    return sizes


def pipelined(voltages, feed_gains, grid_index, decay_rates, delays):
    shards, blocks = lax.axis_size("shard"), lax.axis_size("section")
    frames = voltages.shape[3] // NSAMP
    chans, trials = delays.shape
    feeds = grid_index.shape[0]
    local = chans // shards
    place = lax.axis_index("shard").reshape(1)
    section = lax.axis_index("section").reshape(1)
    sizes = [32, 64, 32]
    starts = [sum(sizes[:c]) for c in range(len(sizes))]
    rows = spectral_constant(chans).reshape(2, shards, local, NSAMP)
    scale = np.float32(1.0 / (frames * feeds))

    far, near = slots(shards)[: shards // 2], slots(shards)[shards // 2 :]

    def exchange(parts, partners):
        return [
            lax.ppermute(part, "shard", [(j, j ^ m) for j in range(shards)]) if m else part
            for part, m in zip(parts, partners)
        ]

    def send_spectra(c, after):
        table = np.ascontiguousarray(rows[:, :, starts[c] : starts[c] + sizes[c]].transpose(1, 0, 2, 3))
        table = jnp.asarray(table.reshape(-1, NSAMP))
        parts, token = channelize(place, table, voltages, sizes[c], shards, after)
        return exchange(parts, far + near), token

    columns = [shards * at for at in starts]

    def make_phases(token):
        by_shard = ((delays + token[0, 0]) & (frames - 1)).reshape(shards, local, trials)
        by_chunk = [by_shard[:, at : at + size].reshape(-1, trials) for at, size in zip(starts, sizes)]
        return phase_tables(jnp.transpose(jnp.concatenate(by_chunk)), frames)

    count = len(sizes)
    received, modulated = {}, {}
    phases = None

    received[0], token = send_spectra(0, [])
    received[1], token = send_spectra(1, [token])
    table = beam_table(grid_index + token[0, 0])
    half, late = shards // 2, []
    for c in range(count):
        start, size = starts[c], sizes[c]
        last = c + 1 == count
        ahead = modulated[c - 1] if 0 < c < count - 1 else []
        sums, level = form_beams(place, feed_gains, table, received[c], start, size, frames, [token] + ahead)
        levels = lax.all_gather(level, "section")
        decay = decay_rates[start : start + size].reshape(size, 1)
        if not last:
            ready, token = normalise(section, levels, decay, sums[:half], scale, [])
            modulated[c] = exchange(ready, far)
            late.append((c, (levels, decay, sums[half:])))
        else:
            after = modulated[c - 1][:half] if c else []
            ready, token = normalise(section, levels, decay, sums, scale, after)
            modulated[c] = exchange(ready, far + near)
        if last:
            for e, held in late:
                modulated[e] = modulated[e] + exchange(normalise(section, *held, scale, [token])[0], near)
        if c == 0:
            phases = make_phases(token)
            token = phases[0]
        if c + 2 < count:
            received[c + 2], token = send_spectra(c + 2, [token])
    chunks = [modulated[c] for c in reversed(range(count))]
    total = dedisperse(place, *phases, columns[::-1], chunks, np.float32(1.0 / math.sqrt(chans)))
    return total.reshape(1, MODF, trials, 2, feeds // shards)


def plain(voltages, feed_gains, grid_index, decay_rates, delays):
    shards = lax.axis_size("shard")
    chans, trials = delays.shape
    feeds, local_feeds = grid_index.shape[0], voltages.shape[2]
    frames = voltages.shape[3] // NSAMP
    samples = voltages[0].reshape(POL * local_feeds * frames, NSAMP)
    rows = jnp.asarray(spectral_constant(chans).reshape(2 * chans, NSAMP))
    spectra = lax.dot_general(rows, samples, (((1,), (1,)), ((), ())), preferred_element_type=jnp.float32)
    spectra = (spectra * (1.0 / math.sqrt(NSAMP))).astype(jnp.bfloat16)
    spectra = spectra.reshape(2, chans, POL, local_feeds, frames)
    turned = lax.all_to_all(spectra, "shard", split_axis=1, concat_axis=3, tiled=True)
    values = turned.astype(jnp.float32)
    gain = feed_gains.astype(jnp.float32)[:, :, None, :, None]
    calibrated = jnp.stack(
        [gain[0] * values[0] - gain[1] * values[1], gain[0] * values[1] + gain[1] * values[0]]
    ).astype(jnp.bfloat16)
    table = beam_table(grid_index).reshape(2, feeds, feeds // LANES, 2, LANES)
    beams = jnp.einsum("akpfn,afdel->eknpdl", calibrated, table, preferred_element_type=jnp.float32)
    power = jnp.sum(beams * beams, axis=(0, 3)).reshape(-1, frames, feeds)
    levels = jnp.mean(power, axis=(1, 2)) + 1e-06
    gathered = lax.all_gather(levels, "section")
    dividend, divisor = jnp.zeros_like(levels), jnp.zeros_like(levels)
    for block in range(gathered.shape[0]):
        later = block <= lax.axis_index("section")
        dividend = jnp.where(later, decay_rates * dividend + gathered[block], dividend)
        divisor = jnp.where(later, decay_rates * divisor + 1.0, divisor)
    power = power * (divisor / dividend)[:, None, None]
    sums = jnp.stack(frame_sums([power[:, n] for n in range(frames)])).astype(jnp.bfloat16)
    moved = lax.all_to_all(sums, "shard", split_axis=2, concat_axis=1, tiled=True)
    turn = jnp.arange(1, MODF + 1, dtype=jnp.int32)[:, None, None] * (delays & (frames - 1))[None]
    cosine = cosine_of(turn, frames).astype(jnp.bfloat16)
    sine = cosine_of(turn - frames // 4, frames).astype(jnp.bfloat16)
    dot = functools.partial(jnp.einsum, "fkt,fkb->ftb", preferred_element_type=jnp.float32)
    real, imag = moved[:MODF], moved[MODF:]
    result = jnp.stack(
        [dot(cosine, real) + dot(sine, imag), dot(cosine, imag) - dot(sine, real)], 2
    ) * (1.0 / math.sqrt(chans))
    return result.astype(jnp.bfloat16)[None]


def solution(mesh):
    def shards(voltages, feed_gains, grid_index, decay_rates, delays):
        count = lax.axis_size("shard")
        fits = (
            voltages.shape[2] == LANES
            and grid_index.shape[0] == count * LANES
            and delays.shape[0] % (count * ROWS) == 0
            and voltages.shape[3] == ROWS * NSAMP
            and count & (count - 1) == 0
            and delays.shape[0] // count >= 2 * ROWS
        )
        form = pipelined if fits else plain
        return form(voltages, feed_gains, grid_index, decay_rates, delays)

    in_specs = (P("section", None, "shard", None), P(None, "shard", None), P(), P("shard"), P())
    out_specs = P("section", None, None, None, "shard")
    return jax.shard_map(shards, mesh=mesh, in_specs=in_specs, out_specs=out_specs, check_vma=False)
```
